32 devices in a mesh: parts: 2 (over x), user: 16 (over z, y, core).
Axes of the slice: x: 2, y: 2, z: 4, core: 2. Of those that a mesh axis runs over, the one named last changes fastest.
Arguments:
- user_embed: bfloat16 [64, 65536], P(None, ('parts', 'user')), parts along dimension 1, may hold values from -6 to 6
- item_embed: bfloat16 [64, 4096], P(None, ('parts', 'user')), parts along dimension 1, may hold values from -6 to 6
- adj_tiles: bfloat16 [4096, 128, 128], P(('parts', 'user')), parts along dimension 0, may hold values from -0.09375 to 0.09375
- tile_rows: int32 [4096], P(('parts', 'user')), parts along dimension 0, may hold values from 0 to 15
- tile_cols: int32 [4096], P(('parts', 'user')), parts along dimension 0, may hold values from 0 to 15
- tile_count: int32 [32], P(('parts', 'user')), parts along dimension 0, may hold values from 16 to 128, as said below
- triple_users: int32 [8192], P(('parts', 'user')), parts along dimension 0, may hold values from 0 to 32767, as said below
- triple_pos: int32 [8192], P(('parts', 'user')), parts along dimension 0, may hold values from 0 to 2047
- triple_neg: int32 [8192], P(('parts', 'user')), parts along dimension 0, may hold values from 0 to 2047
Outputs:
- grad_user: float32 [64, 65536], P(None, ('parts', 'user')), parts along dimension 1
- grad_item: float32 [64, 4096], P(None, ('parts', 'user')), parts along dimension 1
The draws below stay inside these ranges and needn't reach their ends.
There are 2 independent parts, one for each index of `parts`. The reference program is written for one: setup_inputs(seed, part) draws one part's arguments, and reference() takes and returns one part's arrays. A program takes and returns all parts, laid end to end along the dimension named above; each array names one. Nothing has to cross between parts.
Inputs may be any that keep to these rules, and one draw needn't show every extreme that they name: The first tile_count[b] slots of block row b are live, the rest ignored; some block row has all 128 slots live in every draw. `triple_users`: triple k names a user of block row k // 256, that is one of users (k // 256) * 16 * 128 to that plus 16 * 128 - 1.
All inputs are finite; a program needn't handle non-finite values.
Results may differ from the reference program's by a relative error of at most 0.004.
Values may be sent and summed in bfloat16 or wider, within the bound.
A program may use at most 64 MiB of HBM per device.

```python
import math
import jax
import jax.numpy as jnp
import numpy as np
from jax import lax

DIM = 64
TS = 128
UB_DEV = 16
TILES_DEV = 128
TRIP_DEV = 256
USERS = 32768
ITEM_BLOCKS = 16
ITEMS = 2048
TILES = 2048
TRIPLES = 4096
N_USER = 16


def draw_tile_count(key, part):
    key = jax.random.fold_in(key, 11)
    first_key, second_key, third_key = jax.random.split(key, 3)
    lower = max(1, TILES_DEV // 8)
    counts = jax.random.randint(first_key, (N_USER,), lower, TILES_DEV // 2 + 1)
    heavy_rows = jax.random.randint(second_key, (N_USER,), 0, 8) == 0
    chosen = jax.random.randint(third_key, (), 0, N_USER)
    full_rows = heavy_rows | (jnp.arange(N_USER) == chosen)
    return jnp.where(full_rows, TILES_DEV, counts).astype(jnp.int32)


def draw_triple_users(key, part):
    key = jax.random.fold_in(key, 23)
    local_ids = jax.random.randint(key, (TRIPLES,), 0, UB_DEV * TS)
    owners = jnp.arange(TRIPLES, dtype=jnp.int32) // TRIP_DEV
    return (local_ids + owners * (UB_DEV * TS)).astype(jnp.int32)


def with_ends(entries, own_key, low, top_value):
    longest = entries.shape.index(max(entries.shape))
    spots = []
    for shift in (0, 1):
        where = [jax.random.randint(jax.random.fold_in(own_key, axis), (), 0, length) for axis, length in enumerate(entries.shape)]
        where[longest] = (where[longest] + shift) % entries.shape[longest]
        spots.append(tuple(where))
    return entries.at[spots[0]].set(low).at[spots[1]].set(top_value)


def shard_levels(key, extent, shards, least, largest):
    level = 1.0
    for position, shards_of in shards:
        steps = jax.random.uniform(jax.random.fold_in(jax.random.fold_in(key, 6), position), (shards_of,), jnp.float32, least / len(shards), largest / len(shards))
        level = level * jnp.repeat(jnp.exp(steps), extent[position] // shards_of).reshape((-1,) + (1,) * (len(extent) - 1 - position))
    return level


def cumulative_ranks(count, skew):
    loads = [(1 << 20) // math.isqrt(grade ** skew) + 1 for grade in range(1, count + 1)]
    scale = 1 + sum(loads) // (1 << 30)
    return np.cumsum(np.array([max(1, weight // scale) for weight in loads]))


def ranked_ids(key, shape, amount, skew):
    listing = cumulative_ranks(amount, skew)
    pick = jax.random.randint(jax.random.fold_in(key, 1), shape, 0, int(listing[amount - 1]))
    grade = jnp.searchsorted(jnp.asarray(listing, jnp.int32), pick, side="right")
    return jax.random.permutation(jax.random.fold_in(key, 2), amount)[grade].astype(jnp.int32)


def centred(stream_key, dims, scale, limit, cuts=(), held_as=jnp.bfloat16):
    factor_of = shard_levels(stream_key, dims, cuts, -0.22, 0.18) if cuts else 1.0
    drawn = jax.random.normal(stream_key, dims, jnp.float32) * scale * factor_of
    return jnp.minimum(jnp.maximum(drawn, -limit), limit).astype(held_as)


def setup_inputs(seed: int = 0, part: int = 0) -> dict:
    key_list = jax.random.split(jax.random.key(seed), 10)
    part_splits = jax.random.split(jax.random.fold_in(key_list[9], part), 10)
    user_embed = centred(part_splits[0], (DIM, USERS), 1.0, 6.0, ((1, 16),))
    item_embed = centred(part_splits[1], (DIM, ITEMS), 1.0, 6.0, ((1, 16),))
    adj_tiles = centred(part_splits[2], (TILES, TS, TS), (TS * TILES_DEV // 4) ** -0.5, 0.09375, ((0, 16),))
    tile_rows = with_ends(jax.random.randint(part_splits[3], (TILES,), 0, UB_DEV), jax.random.fold_in(part_splits[3], 1), 0, UB_DEV - 1).astype(jnp.int32)
    tile_cols = with_ends(jax.random.randint(part_splits[4], (TILES,), 0, ITEM_BLOCKS), jax.random.fold_in(part_splits[4], 1), 0, ITEM_BLOCKS - 1).astype(jnp.int32)
    tile_count = draw_tile_count(jax.random.fold_in(jax.random.fold_in(key_list[9], part), 71), part)
    triple_users = draw_triple_users(jax.random.fold_in(jax.random.fold_in(key_list[9], part), 71), part)
    triple_pos = with_ends(ranked_ids(part_splits[7], (TRIPLES,), ITEMS, 2), jax.random.fold_in(part_splits[7], 3), 0, ITEMS - 1).astype(jnp.int32)
    triple_neg = with_ends(jax.random.randint(part_splits[8], (TRIPLES,), 0, ITEMS), jax.random.fold_in(part_splits[8], 1), 0, ITEMS - 1).astype(jnp.int32)
    return dict(user_embed=user_embed, item_embed=item_embed, adj_tiles=adj_tiles, tile_rows=tile_rows, tile_cols=tile_cols, tile_count=tile_count, triple_users=triple_users, triple_pos=triple_pos, triple_neg=triple_neg)


def block_sum(tiles_dev, read_idx, write_idx, live_count, source, out_blocks, pattern):
    picked = jnp.take(source, read_idx, axis=1)
    product = jnp.einsum(pattern, picked.astype(jnp.float32), tiles_dev.astype(jnp.float32))
    targets = lax.broadcasted_iota(jnp.int32, (1, out_blocks), 1)
    slot_ids = lax.broadcasted_iota(jnp.int32, (read_idx.shape[0], 1), 0)
    placed = ((write_idx[:, None] == targets) & (slot_ids < live_count)).astype(jnp.float32)
    return jnp.einsum("dtx,tb->dbx", product, placed, precision=lax.Precision.HIGHEST)


def reference(user_embed, item_embed, adj_tiles, tile_rows, tile_cols, tile_count, triple_users, triple_pos, triple_neg):
    tiles_all = adj_tiles.reshape(N_USER, TILES_DEV, TS, TS)
    rows_all = tile_rows.reshape(N_USER, TILES_DEV)
    cols_all = tile_cols.reshape(N_USER, TILES_DEV)

    def to_users(item_full):
        source = item_full.reshape(DIM, ITEM_BLOCKS, TS)

        def one_row(pieces):
            tiles_dev, cols_dev, rows_dev, live = pieces
            return block_sum(tiles_dev, cols_dev, rows_dev, live, source, UB_DEV, "dtc,trc->dtr")

        blocks = lax.map(one_row, (tiles_all, cols_all, rows_all, tile_count))
        return blocks.transpose(1, 0, 2, 3).reshape(DIM, USERS)

    def to_items(user_full):
        sources = user_full.reshape(DIM, N_USER, UB_DEV, TS).transpose(1, 0, 2, 3)

        def advance(running, pieces):
            tiles_dev, rows_dev, cols_dev, live, source = pieces
            return running + block_sum(tiles_dev, rows_dev, cols_dev, live, source, ITEM_BLOCKS, "dtr,trc->dtc"), None

        start = jnp.zeros((DIM, ITEM_BLOCKS, TS), jnp.float32)
        running, _ = lax.scan(advance, start, (tiles_all, rows_all, cols_all, tile_count, sources))
        return running.reshape(DIM, ITEMS)

    user_one = to_users(item_embed).astype(jnp.bfloat16)
    item_one = to_items(user_embed).astype(jnp.bfloat16)
    user_two = to_users(item_one)
    item_two = to_items(user_one).astype(jnp.bfloat16)
    user_final = (user_embed.astype(jnp.float32) + user_one.astype(jnp.float32) + user_two) / 3.0
    item_final = (item_embed.astype(jnp.float32) + item_one.astype(jnp.float32) + item_two.astype(jnp.float32)) / 3.0
    user_pick = jnp.take(user_final, triple_users, axis=1)
    pos_pick = jnp.take(item_final, triple_pos, axis=1)
    neg_pick = jnp.take(item_final, triple_neg, axis=1)
    spread = pos_pick - neg_pick
    margin = jnp.sum(user_pick * spread, axis=0)
    slope = -jax.nn.sigmoid(-margin)
    grad_final_u = jnp.zeros((DIM, USERS), jnp.float32).at[:, triple_users].add(slope[None, :] * spread) / 3.0
    item_terms = jnp.zeros((DIM, ITEMS), jnp.float32).at[:, triple_pos].add(slope[None, :] * user_pick)
    item_terms = item_terms.at[:, triple_neg].add(-slope[None, :] * user_pick)
    grad_final_i = item_terms / 3.0
    item_back = (grad_final_i + to_items(grad_final_u.astype(jnp.bfloat16))).astype(jnp.bfloat16)
    user_back = (grad_final_u + to_users(grad_final_i.astype(jnp.bfloat16))).astype(jnp.bfloat16)
    grad_user = grad_final_u + to_users(item_back)
    grad_item = grad_final_i + to_items(user_back)
    return grad_user, grad_item
```

```python
import functools

import jax
import jax.numpy as jnp
from jax import lax
from jax.experimental import pallas as pl
from jax.experimental.pallas import tpu as pltpu
from jax.sharding import PartitionSpec as P

MESH = pl.DeviceIdType.MESH
F32 = jnp.float32
BF16 = jnp.bfloat16


def dot_nn(a, b):
    return jnp.dot(a, b, preferred_element_type=F32)


def dot_nt(a, b):
    return lax.dot_general(a, b, (((1,), (1,)), ((), ())), preferred_element_type=F32)


def split_rows(x):
    high = x.astype(BF16)
    low = (x - high.astype(F32)).astype(BF16)
    return jnp.concatenate([high, low], axis=0)


def join_rows(x):
    half = x.shape[0] // 2
    return x[:half] + x[half:]


def dense_kernel(row_blocks, rows_ref, cols_ref, count_ref, tiles_ref, out_ref, first, follow, acc):
    pair = pl.program_id(0)
    ts = tiles_ref.shape[1]
    slots = tiles_ref.shape[0]
    places = first.shape[0]

    @pl.when(pair == 0)
    def _():
        def clear(i, carry):
            first[i] = -1
            return carry

        lax.fori_loop(0, places, clear, 0, unroll=8)

        def link(s, carry):
            place = cols_ref[s] * row_blocks + rows_ref[s]
            follow[s] = first[place]
            first[place] = s
            return carry

        lax.fori_loop(0, jnp.minimum(count_ref[0], slots), link, 0)

    for half in range(2):
        def fill(r, carry):
            s0 = first[(pair * 2 + half) * row_blocks + r]
            at = pl.ds(pl.multiple_of(r * ts, ts), ts)
            lanes = slice(half * ts, half * ts + ts)

            @pl.when(s0 < 0)
            def _():
                out_ref[0, at, lanes] = jnp.zeros((ts, ts), BF16)

            @pl.when(s0 >= 0)
            def _():
                s1 = follow[s0]

                @pl.when(s1 < 0)
                def _():
                    out_ref[0, at, lanes] = tiles_ref[s0]

                @pl.when(s1 >= 0)
                def _():
                    acc[...] = tiles_ref[s0].astype(F32)

                    def more(s):
                        acc[...] += tiles_ref[s].astype(F32)
                        return follow[s]

                    lax.while_loop(lambda s: s >= 0, more, s1)
                    out_ref[0, at, lanes] = acc[...].astype(BF16)

            return carry

        lax.fori_loop(0, row_blocks, fill, 0)


def dense_rows(adj_tiles, tile_rows, tile_cols, tile_count, user_dev, item_all):
    slots, ts, _ = adj_tiles.shape
    row_blocks = user_dev // ts
    pairs = item_all // (2 * ts)
    return pl.pallas_call(
        functools.partial(dense_kernel, row_blocks),
        grid_spec=pltpu.PrefetchScalarGridSpec(
            num_scalar_prefetch=3,
            grid=(pairs,),
            in_specs=[pl.BlockSpec((slots, ts, ts), lambda j, *_: (0, 0, 0))],
            out_specs=pl.BlockSpec((1, user_dev, 2 * ts), lambda j, *_: (j, 0, 0)),
            scratch_shapes=[
                pltpu.SMEM((row_blocks * pairs * 2,), jnp.int32),
                pltpu.SMEM((slots,), jnp.int32),
                pltpu.VMEM((ts, ts), F32),
            ],
        ),
        out_shape=jax.ShapeDtypeStruct((pairs, user_dev, 2 * ts), BF16),
        compiler_params=pltpu.CompilerParams(vmem_limit_bytes=24 << 20),
    )(tile_rows, tile_cols, tile_count, adj_tiles)


def main_kernel(
    n,
    ue_ref, ie_ref, tu_ref, tp_ref, tn_ref, r_hbm,
    gu_ref, gi_ref,
    rmat, part, twin_in, send_low, recv_low, gather, u_one, u_sum, u_back, grad_low,
    u_pick_hot, u_put_hot, i_pick_hot, i_put_hot, pick, item_hl, shards,
    load_sem, rs_tsend, rs_trecv, rs_send, rs_recv, ag_send, ag_recv, ag_tsend, ag_trecv,
):
    h = n // 2
    me = lax.axis_index("user")
    core = lax.rem(me, 2)
    spot = lax.div(me, 2)
    twin = me + 1 - 2 * core
    user_dev = ue_ref.shape[1]
    wide = rmat.shape[2]
    half = wide // 2
    chunks = user_dev // wide
    trips = tu_ref.shape[1]

    def peer(k):
        return lax.rem(spot + k, h)

    def source(k):
        return lax.rem(spot + h - k, h)

    def device(q):
        return {"user": 2 * q + core}

    barrier = pltpu.get_barrier_semaphore()
    pl.semaphore_signal(barrier, inc=1, device_id={"user": twin}, device_id_type=MESH)

    def greet(k, carry):
        pl.semaphore_signal(barrier, inc=1, device_id=device(peer(k)), device_id_type=MESH)
        return carry

    lax.fori_loop(1, h, greet, 0)

    def load_copy(j):
        return pltpu.make_async_copy(r_hbm.at[j], rmat.at[j], load_sem.at[j])

    def load_start(j, carry):
        load_copy(j).start()
        return carry

    lax.fori_loop(0, h, load_start, 0)

    def ag_copy(g, sem, k, q):
        return pltpu.make_async_remote_copy(
            src_ref=gather.at[g, core, q], dst_ref=gather.at[g, core, q],
            send_sem=ag_send.at[sem, k], recv_sem=ag_recv.at[sem, k],
            device_id=device(peer(k)), device_id_type=MESH)

    def ag_twin(g, sem, k):
        q = source(k)
        return pltpu.make_async_remote_copy(
            src_ref=gather.at[g, core, q], dst_ref=gather.at[g, core, q],
            send_sem=ag_tsend.at[sem, k], recv_sem=ag_trecv.at[sem, k],
            device_id={"user": twin}, device_id_type=MESH)

    def ag_start(g, sem, value):
        gather[g, core, spot] = value

        def go(k, carry):
            ag_copy(g, sem, k, spot).start()
            return carry

        lax.fori_loop(1, h, go, 0)
        ag_twin(g, sem, 0).start()

    def ag_forward(g, sem):
        def go(k, carry):
            pltpu.make_async_remote_copy(
                src_ref=gather.at[g, core, source(k)], dst_ref=gather.at[g, core, source(k)],
                send_sem=ag_send.at[sem, k], recv_sem=ag_recv.at[sem, k],
                device_id=device(peer(k)), device_id_type=MESH).wait_recv()
            ag_twin(g, sem, k).start()
            return carry

        lax.fori_loop(1, h, go, 0)

    def ag_finish(g, sem):
        def go(k, carry):
            q = source(k)
            pltpu.make_async_remote_copy(
                src_ref=gather.at[g, core, q], dst_ref=gather.at[g, 1 - core, q],
                send_sem=ag_tsend.at[sem, k], recv_sem=ag_trecv.at[sem, k],
                device_id={"user": twin}, device_id_type=MESH).wait_recv()
            ag_twin(g, sem, k).wait_send()
            return carry

        lax.fori_loop(0, h, go, 0)

        def done(k, carry):
            ag_copy(g, sem, k, spot).wait_send()
            return carry

        lax.fori_loop(1, h, done, 0)

    def rs_twin(p, sem):
        return pltpu.make_async_remote_copy(
            src_ref=part.at[p, 1 - core], dst_ref=twin_in.at[p],
            send_sem=rs_tsend.at[sem], recv_sem=rs_trecv.at[sem],
            device_id={"user": twin}, device_id_type=MESH)

    def rs_copy(p, sem, k):
        return pltpu.make_async_remote_copy(
            src_ref=send_low.at[p, k], dst_ref=recv_low.at[p, k],
            send_sem=rs_send.at[sem, k], recv_sem=rs_recv.at[sem, k],
            device_id=device(peer(k)), device_id_type=MESH)

    def rs_second(p, sem):
        rs_twin(p, sem).wait_recv()

        def go(k, carry):
            q = peer(k)
            send_low[p, k] = (part[p, core, q] + twin_in[p, q]).astype(BF16)
            rs_copy(p, sem, k).start()
            return carry

        lax.fori_loop(1, h, go, 0)

    def rs_finish(p, sem):
        shards[...] = part[p, core, spot] + twin_in[p, spot]

        def go(k, carry):
            rs_copy(p, sem, k).wait_recv()
            shards[...] += recv_low[p, k].astype(F32)
            return carry

        lax.fori_loop(1, h, go, 0)

        def done(k, carry):
            rs_copy(p, sem, k).wait_send()
            return carry

        lax.fori_loop(1, h, done, 0)
        rs_twin(p, sem).wait_send()
        return shards[...]

    def both(g, j):
        return jnp.concatenate([gather[g, 0, j], gather[g, 1, j]], axis=1)

    def to_items(src_ref, p, loading=False):
        def go(j, carry):
            if loading:
                load_copy(j).wait()
            out = dot_nn(src_ref[...], rmat[j])
            part[p, 0, j] = out[:, :half]
            part[p, 1, j] = out[:, half:]
            return carry

        lax.fori_loop(0, h, go, 0)

    def at_chunk(r):
        return pl.ds(pl.multiple_of(r * wide, wide), wide)

    def to_users(g, r):
        at = at_chunk(r)
        total = dot_nt(both(g, 0), rmat[0, at, :])
        for j in range(1, h):
            total += dot_nt(both(g, j), rmat[j, at, :])
        return total

    def loop_users(step):
        def go(r, carry):
            step(r, at_chunk(r))
            return carry

        lax.fori_loop(0, chunks, go, 0)

    pl.semaphore_wait(barrier, h)
    ag_start(0, 0, ie_ref[...])
    to_items(ue_ref, 0, loading=True)
    rs_twin(0, 0).start()
    ag_forward(0, 0)
    rs_second(0, 0)
    ag_finish(0, 0)

    def step_one(r, at):
        u_one[:, at] = to_users(0, r).astype(BF16)

    loop_users(step_one)
    item_one = rs_finish(0, 0)
    ag_start(1, 1, item_one.astype(BF16))
    to_items(u_one, 1)
    rs_twin(1, 1).start()
    ag_forward(1, 1)
    rs_second(1, 1)

    local = tu_ref[...] - me * user_dev

    def as_column(row):
        return jnp.transpose(jnp.broadcast_to(row, (128, trips)))

    def hot(mask):
        return jnp.where(mask, 1.0, 0.0)

    def build(j, carry):
        down = lax.broadcasted_iota(jnp.int32, (wide, trips), 0) + j * wide
        i_pick_hot[j] = (hot(down == tp_ref[...]) - hot(down == tn_ref[...])).astype(BF16)
        for s in range(wide // 128):
            along = lax.broadcasted_iota(jnp.int32, (trips, 128), 1) + (j * wide + s * 128)
            i_put_hot[j, :, s * 128:(s + 1) * 128] = (
                hot(along == as_column(tp_ref[...])) - hot(along == as_column(tn_ref[...]))
            ).astype(BF16)
        return carry

    def build_users(j, carry):
        down = lax.broadcasted_iota(jnp.int32, (wide, trips), 0) + j * wide
        u_pick_hot[j] = hot(down == local).astype(BF16)
        for s in range(wide // 128):
            along = lax.broadcasted_iota(jnp.int32, (trips, 128), 1) + (j * wide + s * 128)
            u_put_hot[j, :, s * 128:(s + 1) * 128] = hot(along == as_column(local)).astype(BF16)
        return carry

    lax.fori_loop(0, chunks, build_users, 0)
    ag_finish(1, 1)
    pick[...] = jnp.zeros_like(pick)

    def step_two(r, at):
        final = (ue_ref[:, at].astype(F32) + u_one[:, at].astype(F32) + to_users(1, r)) / 3.0
        pick[...] += join_rows(dot_nn(split_rows(final), u_pick_hot[r]))

    loop_users(step_two)
    item_two = rs_finish(1, 1)
    ag_start(2, 2, item_two.astype(BF16))
    lax.fori_loop(0, h, build, 0)
    ag_forward(2, 2)
    ag_finish(2, 2)

    u_pick = pick[...]

    item_hl[...] = jnp.zeros_like(item_hl)

    def step_spread(j, carry):
        final = (both(0, j).astype(F32) + both(1, j).astype(F32) + both(2, j).astype(F32)) / 3.0
        item_hl[...] += dot_nn(split_rows(final), i_pick_hot[j])
        return carry

    lax.fori_loop(0, h, step_spread, 0)
    spread = join_rows(item_hl[...])
    margin = jnp.sum(u_pick * spread, axis=0, keepdims=True)
    slope = -jax.nn.sigmoid(-margin)
    item_hl[...] = split_rows(slope * u_pick).astype(F32)

    def step_terms(j, carry):
        out = join_rows(dot_nn(item_hl[...].astype(BF16), i_put_hot[j])) / 3.0
        part[0, 0, j] = out[:, :half]
        part[0, 1, j] = out[:, half:]
        return carry

    lax.fori_loop(0, h, step_terms, 0)
    rs_twin(0, 0).start()
    item_hl[...] = split_rows(slope * spread).astype(F32)

    def step_grad(r, at):
        out = join_rows(dot_nn(item_hl[...].astype(BF16), u_put_hot[r])) / 3.0
        u_sum[:, at] = out
        grad_low[:, at] = out.astype(BF16)

    loop_users(step_grad)
    rs_second(0, 0)
    to_items(grad_low, 1)
    rs_twin(1, 1).start()
    grad_shard = rs_finish(0, 0)
    ag_start(0, 0, grad_shard.astype(BF16))
    pick[:, 0:half] = grad_shard
    rs_second(1, 1)
    ag_forward(0, 0)
    ag_finish(0, 0)

    def step_back(r, at):
        u_back[:, at] = (u_sum[:, at] + to_users(0, r)).astype(BF16)

    loop_users(step_back)
    back = rs_finish(1, 1)
    ag_start(1, 1, (pick[:, 0:half] + back).astype(BF16))
    to_items(u_back, 0)
    rs_twin(0, 0).start()
    ag_forward(1, 1)
    rs_second(0, 0)
    ag_finish(1, 1)

    def step_out(r, at):
        gu_ref[:, at] = u_sum[:, at] + to_users(1, r)

    loop_users(step_out)
    gi_ref[...] = pick[:, 0:half] + rs_finish(0, 0)


def shards(
    user_embed, item_embed, adj_tiles, tile_rows, tile_cols, tile_count,
    triple_users, triple_pos, triple_neg,
):
    n = lax.axis_size("user")
    h = n // 2
    features, user_dev = user_embed.shape
    item_dev = item_embed.shape[1]
    wide = 2 * item_dev
    trips = triple_users.shape[0]
    chunks = user_dev // wide
    rmat = dense_rows(adj_tiles, tile_rows, tile_cols, tile_count, user_dev, item_dev * n)
    vmem = pl.BlockSpec(memory_space=pltpu.VMEM)
    dma = pltpu.SemaphoreType.DMA
    need = rmat.size * 2 + (24 << 20)
    return pl.pallas_call(
        functools.partial(main_kernel, n),
        out_shape=(
            jax.ShapeDtypeStruct((features, user_dev), F32),
            jax.ShapeDtypeStruct((features, item_dev), F32),
        ),
        in_specs=[vmem] * 5 + [pl.BlockSpec(memory_space=pl.ANY)],
        out_specs=(vmem, vmem),
        scratch_shapes=[
            pltpu.VMEM(rmat.shape, BF16),
            pltpu.VMEM((2, 2, h, features, item_dev), F32),
            pltpu.VMEM((2, h, features, item_dev), F32),
            pltpu.VMEM((2, h, features, item_dev), BF16),
            pltpu.VMEM((2, h, features, item_dev), BF16),
            pltpu.VMEM((3, 2, h, features, item_dev), BF16),
            pltpu.VMEM((features, user_dev), BF16),
            pltpu.VMEM((features, user_dev), F32),
            pltpu.VMEM((features, user_dev), BF16),
            pltpu.VMEM((features, user_dev), BF16),
            pltpu.VMEM((chunks, wide, trips), BF16),
            pltpu.VMEM((chunks, trips, wide), BF16),
            pltpu.VMEM((h, wide, trips), BF16),
            pltpu.VMEM((h, trips, wide), BF16),
            pltpu.VMEM((features, trips), F32),
            pltpu.VMEM((2 * features, trips), F32),
            pltpu.VMEM((features, item_dev), F32),
            dma((h,)),
            dma((2,)), dma((2,)), dma((2, h)), dma((2, h)),
            dma((3, h)), dma((3, h)), dma((3, h)), dma((3, h)),
        ],
        compiler_params=pltpu.CompilerParams(
            collective_id=0, has_side_effects=True, vmem_limit_bytes=min(need, 60 << 20)
        ),
    )(
        user_embed, item_embed,
        triple_users.reshape(1, trips), triple_pos.reshape(1, trips), triple_neg.reshape(1, trips),
        rmat,
    )


def solution(mesh):
    split = P(("parts", "user"))
    columns = P(None, ("parts", "user"))
    return jax.shard_map(
        shards,
        mesh=mesh,
        in_specs=(columns, columns, P(("parts", "user"), None, None)) + (split,) * 6,
        out_specs=(columns, columns),
        check_vma=False,
    )
```

```python
import functools
import math

import jax
import jax.numpy as jnp
from jax import lax
from jax.experimental import pallas as pl
from jax.experimental.pallas import tpu as pltpu
from jax.sharding import PartitionSpec as P

MESH = pl.DeviceIdType.MESH
F32 = jnp.float32
BF16 = jnp.bfloat16


def dot_nn(a, b):
    return jnp.dot(a, b, preferred_element_type=F32)


def dot_nt(a, b):
    return lax.dot_general(a, b, (((1,), (1,)), ((), ())), preferred_element_type=F32)


def split_rows(x):
    high = x.astype(BF16)
    low = (x - high.astype(F32)).astype(BF16)
    return jnp.concatenate([high, low], axis=0)


def join_rows(x):
    half = x.shape[0] // 2
    return x[:half] + x[half:]


def dense_kernel(rows_ref, cols_ref, count_ref, tiles_ref, out_ref, first, follow, shared):
    slots, ts, _ = tiles_ref.shape
    item_blocks, row_blocks = out_ref.shape[:2]

    def clear(c, carry):
        for r in range(row_blocks):
            first[c * row_blocks + r] = -1
            out_ref[c, r] = jnp.zeros((ts, ts), BF16)
        return carry

    lax.fori_loop(0, item_blocks, clear, 0)

    def link(s, crowded):
        c, r = cols_ref[s], rows_ref[s]
        place = c * row_blocks + r
        head = first[place]

        @pl.when(head < 0)
        def _():
            first[place] = s
            follow[s] = -1
            out_ref[c, r] = tiles_ref[s]

        @pl.when(head >= 0)
        def _():
            after = follow[head]
            follow[s] = after
            follow[head] = s
            shared[crowded] = place

        fresh = (head >= 0) & (follow[s] < 0)
        return crowded + fresh.astype(jnp.int32)

    crowded = lax.fori_loop(0, jnp.minimum(count_ref[0], slots), link, 0)

    def merge(i, carry):
        place = shared[i]
        c, r = lax.div(place, row_blocks), lax.rem(place, row_blocks)
        s1 = follow[first[place]]
        s2 = follow[s1]
        total = out_ref[c, r].astype(F32) + tiles_ref[s1].astype(F32)

        @pl.when(s2 < 0)
        def _():
            out_ref[c, r] = total.astype(BF16)

        @pl.when(s2 >= 0)
        def _():
            def more(pair):
                return follow[pair[0]], pair[1] + tiles_ref[pair[0]].astype(F32)

            out_ref[c, r] = lax.while_loop(lambda pair: pair[0] >= 0, more, (s2, total))[1].astype(BF16)

        return carry

    lax.fori_loop(0, crowded, merge, 0)


def dense_rows(adj_tiles, tile_rows, tile_cols, tile_count, user_dev, item_all):
    slots, ts, _ = adj_tiles.shape
    shape = (item_all // ts, user_dev // ts, ts, ts)
    smem = pl.BlockSpec(memory_space=pltpu.SMEM)
    vmem = pl.BlockSpec(memory_space=pltpu.VMEM)
    return pl.pallas_call(
        dense_kernel,
        in_specs=[smem, smem, smem, vmem],
        out_specs=vmem,
        scratch_shapes=[
            pltpu.SMEM((shape[0] * shape[1],), jnp.int32),
            pltpu.SMEM((slots,), jnp.int32),
            pltpu.SMEM((slots + 1,), jnp.int32),
        ],
        out_shape=jax.ShapeDtypeStruct(shape, BF16),
        compiler_params=pltpu.CompilerParams(
            vmem_limit_bytes=math.prod(shape) * 2 + adj_tiles.size * 2 + (2 << 20)
        ),
    )(tile_rows, tile_cols, tile_count, adj_tiles)


def main_kernel(
    n,
    ue_ref, ie_ref, tu_ref, tp_ref, tn_ref, rmat,
    gu_ref, gi_ref,
    part, twin_in, send_low, recv_low, gather, u_one, u_sum, u_back, grad_low,
    u_pick_hot, u_put_hot, i_pick_hot, i_put_hot, pick, item_hl, shards, columns,
    rs_tsend, rs_trecv, rs_send, rs_recv, ag_send, ag_recv, ag_tsend, ag_trecv,
):
    h = n // 2
    me = lax.axis_index("user")
    core = lax.rem(me, 2)
    spot = lax.div(me, 2)
    twin = me + 1 - 2 * core
    user_dev = ue_ref.shape[1]
    half = rmat.shape[3]
    wide = 2 * half
    chunks = user_dev // wide
    trips = tu_ref.shape[1]

    def peer(k):
        return lax.rem(spot + k, h)

    def source(k):
        return lax.rem(spot + h - k, h)

    def device(q):
        return {"user": 2 * q + core}

    barrier = pltpu.get_barrier_semaphore()
    pl.semaphore_signal(barrier, inc=1, device_id={"user": twin}, device_id_type=MESH)

    def greet(k, carry):
        pl.semaphore_signal(barrier, inc=1, device_id=device(peer(k)), device_id_type=MESH)
        return carry

    lax.fori_loop(1, h, greet, 0)

    def ag_copy(g, sem, k, q):
        return pltpu.make_async_remote_copy(
            src_ref=gather.at[g, core, q], dst_ref=gather.at[g, core, q],
            send_sem=ag_send.at[sem, k], recv_sem=ag_recv.at[sem, k],
            device_id=device(peer(k)), device_id_type=MESH)

    def ag_twin(g, sem, k):
        q = source(k)
        return pltpu.make_async_remote_copy(
            src_ref=gather.at[g, core, q], dst_ref=gather.at[g, core, q],
            send_sem=ag_tsend.at[sem, k], recv_sem=ag_trecv.at[sem, k],
            device_id={"user": twin}, device_id_type=MESH)

    def ag_start(g, sem, value):
        gather[g, core, spot] = value

        def go(k, carry):
            ag_copy(g, sem, k, spot).start()
            return carry

        lax.fori_loop(1, h, go, 0)
        ag_twin(g, sem, 0).start()

    def ag_forward(g, sem):
        def go(k, carry):
            pltpu.make_async_remote_copy(
                src_ref=gather.at[g, core, source(k)], dst_ref=gather.at[g, core, source(k)],
                send_sem=ag_send.at[sem, k], recv_sem=ag_recv.at[sem, k],
                device_id=device(peer(k)), device_id_type=MESH).wait_recv()
            ag_twin(g, sem, k).start()
            return carry

        lax.fori_loop(1, h, go, 0)

    def ag_finish(g, sem):
        def go(k, carry):
            q = source(k)
            pltpu.make_async_remote_copy(
                src_ref=gather.at[g, core, q], dst_ref=gather.at[g, 1 - core, q],
                send_sem=ag_tsend.at[sem, k], recv_sem=ag_trecv.at[sem, k],
                device_id={"user": twin}, device_id_type=MESH).wait_recv()
            ag_twin(g, sem, k).wait_send()
            return carry

        lax.fori_loop(0, h, go, 0)

        def done(k, carry):
            ag_copy(g, sem, k, spot).wait_send()
            return carry

        lax.fori_loop(1, h, done, 0)

    def rs_twin(p, sem):
        return pltpu.make_async_remote_copy(
            src_ref=part.at[p, 1 - core], dst_ref=twin_in.at[p],
            send_sem=rs_tsend.at[sem], recv_sem=rs_trecv.at[sem],
            device_id={"user": twin}, device_id_type=MESH)

    def rs_copy(p, sem, k):
        return pltpu.make_async_remote_copy(
            src_ref=send_low.at[p, k], dst_ref=recv_low.at[p, k],
            send_sem=rs_send.at[sem, k], recv_sem=rs_recv.at[sem, k],
            device_id=device(peer(k)), device_id_type=MESH)

    def rs_second(p, sem):
        rs_twin(p, sem).wait_recv()

        def go(k, carry):
            q = peer(k)
            send_low[p, k] = (part[p, core, q] + twin_in[p, q]).astype(BF16)
            rs_copy(p, sem, k).start()
            return carry

        lax.fori_loop(1, h, go, 0)

    def rs_finish(p, sem):
        shards[...] = part[p, core, spot] + twin_in[p, spot]

        def go(k, carry):
            rs_copy(p, sem, k).wait_recv()
            shards[...] += recv_low[p, k].astype(F32)
            return carry

        lax.fori_loop(1, h, go, 0)

        def done(k, carry):
            rs_copy(p, sem, k).wait_send()
            return carry

        lax.fori_loop(1, h, done, 0)
        rs_twin(p, sem).wait_send()
        return shards[...]

    def both(g, j):
        return jnp.concatenate([gather[g, 0, j], gather[g, 1, j]], axis=1)

    def to_items(src_ref, p):
        def go(j, carry):
            out = dot_nn(src_ref[...], jnp.concatenate(
                [rmat[2 * j].reshape(user_dev, half), rmat[2 * j + 1].reshape(user_dev, half)], axis=1))
            part[p, 0, j] = out[:, :half]
            part[p, 1, j] = out[:, half:]
            return carry

        lax.fori_loop(0, h, go, 0, unroll=4)

    def at_chunk(r):
        return pl.ds(pl.multiple_of(r * wide, wide), wide)

    def to_users(g, r):
        total = None
        for j in range(h):
            left = rmat[2 * j, pl.ds(2 * r, 2)].reshape(wide, half)
            right = rmat[2 * j + 1, pl.ds(2 * r, 2)].reshape(wide, half)
            term = dot_nt(both(g, j), jnp.concatenate([left, right], axis=1))
            total = term if total is None else total + term
        return total

    def loop_users(step):
        def go(r, carry):
            step(r, at_chunk(r))
            return carry

        lax.fori_loop(0, chunks, go, 0, unroll=4)

    local = tu_ref[...] - me * user_dev

    def as_column(row):
        return jnp.transpose(jnp.broadcast_to(row, (128, trips)))

    def hot(mask):
        return jnp.where(mask, 1.0, 0.0)

    def build(j, carry):
        down = lax.broadcasted_iota(jnp.int32, (wide, trips), 0) + j * wide
        i_pick_hot[j] = (hot(down == tp_ref[...]) - hot(down == tn_ref[...])).astype(BF16)
        for s in range(wide // 128):
            along = lax.broadcasted_iota(jnp.int32, (trips, 128), 1) + (j * wide + s * 128)
            i_put_hot[j, :, s * 128:(s + 1) * 128] = (
                hot(along == columns[1]) - hot(along == columns[2])
            ).astype(BF16)
        return carry

    def build_users(j, carry):
        down = lax.broadcasted_iota(jnp.int32, (wide, trips), 0) + j * wide
        u_pick_hot[j] = hot(down == local).astype(BF16)
        for s in range(wide // 128):
            along = lax.broadcasted_iota(jnp.int32, (trips, 128), 1) + (j * wide + s * 128)
            u_put_hot[j, :, s * 128:(s + 1) * 128] = hot(along == columns[0]).astype(BF16)
        return carry

    pl.semaphore_wait(barrier, h)
    ag_start(0, 0, ie_ref[...])
    to_items(ue_ref, 0)
    rs_twin(0, 0).start()
    columns[0] = as_column(local)
    columns[1] = as_column(tp_ref[...])
    columns[2] = as_column(tn_ref[...])
    lax.fori_loop(0, chunks, build_users, 0)
    rs_second(0, 0)
    ag_forward(0, 0)
    lax.fori_loop(0, h, build, 0)
    ag_finish(0, 0)

    def step_one(r, at):
        u_one[:, at] = to_users(0, r).astype(BF16)

    loop_users(step_one)
    item_one = rs_finish(0, 0)
    ag_start(1, 1, item_one.astype(BF16))
    to_items(u_one, 1)
    rs_twin(1, 1).start()
    rs_second(1, 1)
    ag_forward(1, 1)
    ag_finish(1, 1)
    item_two = rs_finish(1, 1)
    ag_start(2, 2, item_two.astype(BF16))
    pick[...] = jnp.zeros_like(pick)

    def step_two(r, at):
        final = (ue_ref[:, at].astype(F32) + u_one[:, at].astype(F32) + to_users(1, r)) / 3.0
        pick[...] += join_rows(dot_nn(split_rows(final), u_pick_hot[r]))

    loop_users(step_two)
    ag_forward(2, 2)
    ag_finish(2, 2)

    u_pick = pick[...]

    item_hl[...] = jnp.zeros_like(item_hl)

    def step_spread(j, carry):
        final = (both(0, j).astype(F32) + both(1, j).astype(F32) + both(2, j).astype(F32)) / 3.0
        item_hl[...] += dot_nn(split_rows(final), i_pick_hot[j])
        return carry

    lax.fori_loop(0, h, step_spread, 0, unroll=8)
    spread = join_rows(item_hl[...])
    margin = jnp.sum(u_pick * spread, axis=0, keepdims=True)
    slope = -jax.nn.sigmoid(-margin)
    item_hl[...] = split_rows(slope * u_pick).astype(F32)

    def step_terms(j, carry):
        out = join_rows(dot_nn(item_hl[...].astype(BF16), i_put_hot[j])) / 3.0
        part[0, 0, j] = out[:, :half]
        part[0, 1, j] = out[:, half:]
        return carry

    lax.fori_loop(0, h, step_terms, 0, unroll=8)
    rs_twin(0, 0).start()
    item_hl[...] = split_rows(slope * spread).astype(F32)

    def step_grad(r, at):
        out = join_rows(dot_nn(item_hl[...].astype(BF16), u_put_hot[r])) / 3.0
        u_sum[:, at] = out
        grad_low[:, at] = out.astype(BF16)

    lax.fori_loop(0, chunks, lambda r, c: (step_grad(r, at_chunk(r)), c)[1], 0, unroll=8)
    rs_second(0, 0)
    to_items(grad_low, 1)
    rs_twin(1, 1).start()
    grad_shard = rs_finish(0, 0)
    ag_start(0, 0, grad_shard.astype(BF16))
    pick[:, 0:half] = grad_shard
    rs_second(1, 1)
    ag_forward(0, 0)
    back = rs_finish(1, 1)
    ag_start(1, 1, (pick[:, 0:half] + back).astype(BF16))
    ag_finish(0, 0)

    def step_back(r, at):
        u_back[:, at] = (u_sum[:, at] + to_users(0, r)).astype(BF16)

    loop_users(step_back)
    to_items(u_back, 0)
    rs_twin(0, 0).start()
    ag_forward(1, 1)
    rs_second(0, 0)
    ag_finish(1, 1)

    def step_out(r, at):
        gu_ref[:, at] = u_sum[:, at] + to_users(1, r)

    loop_users(step_out)
    gi_ref[...] = pick[:, 0:half] + rs_finish(0, 0)


def shards(
    user_embed, item_embed, adj_tiles, tile_rows, tile_cols, tile_count,
    triple_users, triple_pos, triple_neg,
):
    n = lax.axis_size("user")
    h = n // 2
    features, user_dev = user_embed.shape
    item_dev = item_embed.shape[1]
    wide = 2 * item_dev
    trips = triple_users.shape[0]
    chunks = user_dev // wide
    rmat = dense_rows(adj_tiles, tile_rows, tile_cols, tile_count, user_dev, item_dev * n)
    vmem = pl.BlockSpec(memory_space=pltpu.VMEM)
    dma = pltpu.SemaphoreType.DMA
    most = 56 << 20 if rmat.size > 8 << 20 else 24 << 20
    return pl.pallas_call(
        functools.partial(main_kernel, n),
        out_shape=(
            jax.ShapeDtypeStruct((features, user_dev), F32),
            jax.ShapeDtypeStruct((features, item_dev), F32),
        ),
        in_specs=[vmem] * 6,
        out_specs=(vmem, vmem),
        scratch_shapes=[
            pltpu.VMEM((2, 2, h, features, item_dev), F32),
            pltpu.VMEM((2, h, features, item_dev), F32),
            pltpu.VMEM((2, h, features, item_dev), BF16),
            pltpu.VMEM((2, h, features, item_dev), BF16),
            pltpu.VMEM((3, 2, h, features, item_dev), BF16),
            pltpu.VMEM((features, user_dev), BF16),
            pltpu.VMEM((features, user_dev), F32),
            pltpu.VMEM((features, user_dev), BF16),
            pltpu.VMEM((features, user_dev), BF16),
            pltpu.VMEM((chunks, wide, trips), BF16),
            pltpu.VMEM((chunks, trips, wide), BF16),
            pltpu.VMEM((h, wide, trips), BF16),
            pltpu.VMEM((h, trips, wide), BF16),
            pltpu.VMEM((features, trips), F32),
            pltpu.VMEM((2 * features, trips), F32),
            pltpu.VMEM((features, item_dev), F32),
            pltpu.VMEM((3, trips, 128), jnp.int32),
            dma((2,)), dma((2,)), dma((2, h)), dma((2, h)),
            dma((3, h)), dma((3, h)), dma((3, h)), dma((3, h)),
        ],
        compiler_params=pltpu.CompilerParams(
            collective_id=0, has_side_effects=True, vmem_limit_bytes=most
        ),
    )(
        user_embed, item_embed,
        triple_users.reshape(1, trips), triple_pos.reshape(1, trips), triple_neg.reshape(1, trips),
        rmat,
    )


def solution(mesh):
    split = P(("parts", "user"))
    columns = P(None, ("parts", "user"))
    return jax.shard_map(
        shards,
        mesh=mesh,
        in_specs=(columns, columns, P(("parts", "user"), None, None)) + (split,) * 6,
        out_specs=(columns, columns),
        check_vma=False,
    )
```

```python
import functools
import math

import jax
import jax.numpy as jnp
from jax import lax
from jax.experimental import pallas as pl
from jax.experimental.pallas import tpu as pltpu
from jax.sharding import PartitionSpec as P

MESH = pl.DeviceIdType.MESH
F32 = jnp.float32
BF16 = jnp.bfloat16


def dot_nn(a, b):
    return jnp.dot(a, b, preferred_element_type=F32)


def dot_nt(a, b):
    return lax.dot_general(a, b, (((1,), (1,)), ((), ())), preferred_element_type=F32)


def split_rows(x):
    high = x.astype(BF16)
    low = (x - high.astype(F32)).astype(BF16)
    return jnp.concatenate([high, low], axis=0)


def join_rows(x):
    half = x.shape[0] // 2
    return x[:half] + x[half:]


def dense_kernel(rows_ref, cols_ref, count_ref, tiles_ref, out_ref, first, follow, shared):
    slots, ts, _ = tiles_ref.shape
    item_blocks, row_blocks = out_ref.shape[:2]

    def clear(c, carry):
        for r in range(row_blocks):
            first[c * row_blocks + r] = -1
            out_ref[c, r] = jnp.zeros((ts, ts), BF16)
        return carry

    lax.fori_loop(0, item_blocks, clear, 0)

    def link(s, crowded):
        c, r = cols_ref[s], rows_ref[s]
        place = c * row_blocks + r
        head = first[place]

        @pl.when(head < 0)
        def _():
            first[place] = s
            follow[s] = -1
            out_ref[c, r] = tiles_ref[s]

        @pl.when(head >= 0)
        def _():
            after = follow[head]
            follow[s] = after
            follow[head] = s
            shared[crowded] = place

        fresh = (head >= 0) & (follow[s] < 0)
        return crowded + fresh.astype(jnp.int32)

    crowded = lax.fori_loop(0, jnp.minimum(count_ref[0], slots), link, 0)

    def merge(i, carry):
        place = shared[i]
        c, r = lax.div(place, row_blocks), lax.rem(place, row_blocks)
        s1 = follow[first[place]]
        s2 = follow[s1]
        total = out_ref[c, r].astype(F32) + tiles_ref[s1].astype(F32)

        @pl.when(s2 < 0)
        def _():
            out_ref[c, r] = total.astype(BF16)

        @pl.when(s2 >= 0)
        def _():
            def more(pair):
                return follow[pair[0]], pair[1] + tiles_ref[pair[0]].astype(F32)

            out_ref[c, r] = lax.while_loop(lambda pair: pair[0] >= 0, more, (s2, total))[1].astype(BF16)

        return carry

    lax.fori_loop(0, crowded, merge, 0)


def dense_rows(adj_tiles, tile_rows, tile_cols, tile_count, user_dev, item_all):
    slots, ts, _ = adj_tiles.shape
    shape = (item_all // ts, user_dev // ts, ts, ts)
    smem = pl.BlockSpec(memory_space=pltpu.SMEM)
    vmem = pl.BlockSpec(memory_space=pltpu.VMEM)
    return pl.pallas_call(
        dense_kernel,
        in_specs=[smem, smem, smem, vmem],
        out_specs=vmem,
        scratch_shapes=[
            pltpu.SMEM((shape[0] * shape[1],), jnp.int32),
            pltpu.SMEM((slots,), jnp.int32),
            pltpu.SMEM((slots + 1,), jnp.int32),
        ],
        out_shape=jax.ShapeDtypeStruct(shape, BF16),
        compiler_params=pltpu.CompilerParams(
            vmem_limit_bytes=math.prod(shape) * 2 + adj_tiles.size * 2 + (2 << 20)
        ),
    )(tile_rows, tile_cols, tile_count, adj_tiles)


def main_kernel(
    n,
    ue_ref, ie_ref, tu_ref, tp_ref, tn_ref, rmat,
    gu_ref, gi_ref,
    part, twin_in, send_low, recv_low, gather, u_one, u_sum, u_back, grad_low,
    u_pick_hot, u_put_hot, i_pick_hot, i_put_hot, pick, item_hl, shards, columns,
    rs_tsend, rs_trecv, rs_send, rs_recv, ag_send, ag_recv, ag_tsend, ag_trecv,
):
    h = n // 2
    me = lax.axis_index("user")
    core = lax.rem(me, 2)
    spot = lax.div(me, 2)
    twin = me + 1 - 2 * core
    user_dev = ue_ref.shape[1]
    half = rmat.shape[3]
    wide = 2 * half
    chunks = user_dev // wide
    trips = tu_ref.shape[1]

    def peer(k):
        partner, bit = 0, 1
        while bit < h:
            mine, other = lax.rem(lax.div(spot, bit), 2), lax.rem(lax.div(k, bit), 2)
            partner += bit * (mine + other - 2 * mine * other)
            bit *= 2
        return partner

    source = peer

    def device(q):
        return {"user": 2 * q + core}

    spots = [peer(k) for k in range(h)]
    barrier = pltpu.get_barrier_semaphore()
    pl.semaphore_signal(barrier, inc=1, device_id={"user": twin}, device_id_type=MESH)

    def greet(k, carry):
        pl.semaphore_signal(barrier, inc=1, device_id=device(peer(k)), device_id_type=MESH)
        return carry

    lax.fori_loop(1, h, greet, 0)

    def ag_copy(g, sem, k, q):
        return pltpu.make_async_remote_copy(
            src_ref=gather.at[g, core, q], dst_ref=gather.at[g, core, q],
            send_sem=ag_send.at[sem, k], recv_sem=ag_recv.at[sem, k],
            device_id=device(peer(k)), device_id_type=MESH)

    def ag_twin(g, sem, k):
        q = source(k)
        return pltpu.make_async_remote_copy(
            src_ref=gather.at[g, core, q], dst_ref=gather.at[g, core, q],
            send_sem=ag_tsend.at[sem, k], recv_sem=ag_trecv.at[sem, k],
            device_id={"user": twin}, device_id_type=MESH)

    def ag_start(g, sem, value):
        gather[g, core, spot] = value

        def go(k, carry):
            ag_copy(g, sem, k, spot).start()
            return carry

        lax.fori_loop(1, h, go, 0)
        ag_twin(g, sem, 0).start()

    near = h // 2

    def ag_forward(g, sem, low=1, high=h):
        def go(k, carry):
            q = peer(k)
            pltpu.make_async_remote_copy(
                src_ref=gather.at[g, core, q], dst_ref=gather.at[g, core, q],
                send_sem=ag_send.at[sem, k], recv_sem=ag_recv.at[sem, k],
                device_id=device(q), device_id_type=MESH).wait_recv()
            ag_twin(g, sem, k).start()
            return carry

        lax.fori_loop(low, high, go, 0)

    def ag_arrive(g, sem, low=0, high=h):
        def go(k, carry):
            q = peer(k)
            pltpu.make_async_remote_copy(
                src_ref=gather.at[g, core, q], dst_ref=gather.at[g, 1 - core, q],
                send_sem=ag_tsend.at[sem, k], recv_sem=ag_trecv.at[sem, k],
                device_id={"user": twin}, device_id_type=MESH).wait_recv()
            return carry

        lax.fori_loop(low, high, go, 0)

    def ag_done(g, sem):
        def sent(k, carry):
            ag_twin(g, sem, k).wait_send()
            return carry

        lax.fori_loop(0, h, sent, 0)

        def done(k, carry):
            ag_copy(g, sem, k, spot).wait_send()
            return carry

        lax.fori_loop(1, h, done, 0)

    def ag_finish(g, sem):
        ag_arrive(g, sem)
        ag_done(g, sem)

    def rs_twin(p, sem, piece):
        span = pl.ds(piece * near, near)
        return pltpu.make_async_remote_copy(
            src_ref=part.at[p, 1 - core, span], dst_ref=twin_in.at[p, span],
            send_sem=rs_tsend.at[sem, piece], recv_sem=rs_trecv.at[sem, piece],
            device_id={"user": twin}, device_id_type=MESH)

    def rs_copy(p, sem, k):
        return pltpu.make_async_remote_copy(
            src_ref=send_low.at[p, k], dst_ref=recv_low.at[p, k],
            send_sem=rs_send.at[sem, k], recv_sem=rs_recv.at[sem, k],
            device_id=device(peer(k)), device_id_type=MESH)

    def rs_second(p, sem, piece):
        rs_twin(p, sem, piece).wait_recv()

        def go(q, carry):
            k = lax.rem(peer(q), h)

            @pl.when(q != spot)
            def _():
                send_low[p, k] = (part[p, core, q] + twin_in[p, q]).astype(BF16)
                rs_copy(p, sem, k).start()

            return carry

        lax.fori_loop(piece * near, piece * near + near, go, 0)

    def rs_finish(p, sem):
        shards[...] = part[p, core, spot] + twin_in[p, spot]

        def go(k, carry):
            rs_copy(p, sem, k).wait_recv()
            shards[...] += recv_low[p, k].astype(F32)
            return carry

        lax.fori_loop(1, h, go, 0)

        def done(k, carry):
            rs_copy(p, sem, k).wait_send()
            return carry

        lax.fori_loop(1, h, done, 0)
        rs_twin(p, sem, 0).wait_send()
        rs_twin(p, sem, 1).wait_send()
        return shards[...]

    def both(g, j):
        return jnp.concatenate([gather[g, 0, j], gather[g, 1, j]], axis=1)

    def to_items(src_ref, p):
        def go(j, carry):
            out = dot_nn(src_ref[...], jnp.concatenate(
                [rmat[2 * j].reshape(user_dev, half), rmat[2 * j + 1].reshape(user_dev, half)], axis=1))
            part[p, 0, j] = out[:, :half]
            part[p, 1, j] = out[:, half:]
            return carry

        lax.fori_loop(0, near, go, 0, unroll=4)
        rs_twin(p, p, 0).start()
        lax.fori_loop(near, h, go, 0, unroll=4)
        rs_twin(p, p, 1).start()

    def at_chunk(r):
        return pl.ds(pl.multiple_of(r * wide, wide), wide)

    def to_users(g, r, low=0, high=h):
        total = None
        for k in range(low, high):
            j = spots[k]
            left = rmat[2 * j, pl.ds(2 * r, 2)].reshape(wide, half)
            right = rmat[2 * j + 1, pl.ds(2 * r, 2)].reshape(wide, half)
            term = dot_nt(both(g, j), jnp.concatenate([left, right], axis=1))
            total = term if total is None else total + term
        return total

    def loop_users(step):
        def go(r, carry):
            step(r, at_chunk(r))
            return carry

        lax.fori_loop(0, chunks, go, 0, unroll=4)

    local = tu_ref[...] - me * user_dev

    def as_column(row):
        return jnp.transpose(jnp.broadcast_to(row, (128, trips)))

    def hot(mask):
        return jnp.where(mask, 1.0, 0.0)

    def build(j, carry):
        down = lax.broadcasted_iota(jnp.int32, (wide, trips), 0) + j * wide
        i_pick_hot[j] = (hot(down == tp_ref[...]) - hot(down == tn_ref[...])).astype(BF16)
        for s in range(wide // 128):
            along = lax.broadcasted_iota(jnp.int32, (trips, 128), 1) + (j * wide + s * 128)
            i_put_hot[j, :, s * 128:(s + 1) * 128] = (
                hot(along == columns[1]) - hot(along == columns[2])
            ).astype(BF16)
        return carry

    def build_users(j, carry):
        down = lax.broadcasted_iota(jnp.int32, (wide, trips), 0) + j * wide
        u_pick_hot[j] = hot(down == local).astype(BF16)
        for s in range(wide // 128):
            along = lax.broadcasted_iota(jnp.int32, (trips, 128), 1) + (j * wide + s * 128)
            u_put_hot[j, :, s * 128:(s + 1) * 128] = hot(along == columns[0]).astype(BF16)
        return carry

    pl.semaphore_wait(barrier, h)
    ag_start(0, 0, ie_ref[...])
    to_items(ue_ref, 0)
    columns[0] = as_column(local)
    columns[1] = as_column(tp_ref[...])
    columns[2] = as_column(tn_ref[...])
    lax.fori_loop(0, chunks, build_users, 0)
    rs_second(0, 0, 0)
    rs_second(0, 0, 1)
    ag_forward(0, 0)
    lax.fori_loop(0, h, build, 0)
    ag_finish(0, 0)

    def step_one(r, at):
        u_one[:, at] = to_users(0, r).astype(BF16)

    loop_users(step_one)
    item_one = rs_finish(0, 0)
    ag_start(1, 1, item_one.astype(BF16))
    to_items(u_one, 1)
    rs_second(1, 1, 0)
    rs_second(1, 1, 1)
    ag_forward(1, 1)
    ag_finish(1, 1)
    item_two = rs_finish(1, 1)
    ag_start(2, 2, item_two.astype(BF16))
    pick[...] = jnp.zeros_like(pick)

    def step_two(r, at):
        final = (ue_ref[:, at].astype(F32) + u_one[:, at].astype(F32) + to_users(1, r)) / 3.0
        pick[...] += join_rows(dot_nn(split_rows(final), u_pick_hot[r]))

    loop_users(step_two)
    ag_forward(2, 2)
    ag_finish(2, 2)

    u_pick = pick[...]

    item_hl[...] = jnp.zeros_like(item_hl)

    def step_spread(j, carry):
        final = (both(0, j).astype(F32) + both(1, j).astype(F32) + both(2, j).astype(F32)) / 3.0
        item_hl[...] += dot_nn(split_rows(final), i_pick_hot[j])
        return carry

    lax.fori_loop(0, h, step_spread, 0, unroll=8)
    spread = join_rows(item_hl[...])
    margin = jnp.sum(u_pick * spread, axis=0, keepdims=True)
    slope = -jax.nn.sigmoid(-margin)
    item_hl[...] = split_rows(slope * u_pick).astype(F32)

    def step_terms(j, carry):
        out = join_rows(dot_nn(item_hl[...].astype(BF16), i_put_hot[j])) / 3.0
        part[0, 0, j] = out[:, :half]
        part[0, 1, j] = out[:, half:]
        return carry

    lax.fori_loop(0, near, step_terms, 0, unroll=4)
    rs_twin(0, 0, 0).start()
    lax.fori_loop(near, h, step_terms, 0, unroll=4)
    rs_twin(0, 0, 1).start()
    item_hl[...] = split_rows(slope * spread).astype(F32)

    def step_grad(r, at):
        out = join_rows(dot_nn(item_hl[...].astype(BF16), u_put_hot[r])) / 3.0
        u_sum[:, at] = out
        grad_low[:, at] = out.astype(BF16)

    lax.fori_loop(0, chunks, lambda r, c: (step_grad(r, at_chunk(r)), c)[1], 0, unroll=8)
    rs_second(0, 0, 0)
    rs_second(0, 0, 1)
    to_items(grad_low, 1)
    grad_shard = rs_finish(0, 0)
    ag_start(0, 0, grad_shard.astype(BF16))
    pick[:, 0:half] = grad_shard
    rs_second(1, 1, 0)
    rs_second(1, 1, 1)
    ag_forward(0, 0, 1, near)
    ag_arrive(0, 0, 0, near)

    def step_near(r, at):
        gu_ref[:, at] = u_sum[:, at] + to_users(0, r, 0, near)

    loop_users(step_near)
    ag_forward(0, 0, near, h)
    back = rs_finish(1, 1)
    ag_start(1, 1, (pick[:, 0:half] + back).astype(BF16))
    ag_arrive(0, 0, near, h)
    ag_done(0, 0)

    def step_back(r, at):
        u_back[:, at] = (gu_ref[:, at] + to_users(0, r, near, h)).astype(BF16)

    loop_users(step_back)
    to_items(u_back, 0)
    rs_second(0, 0, 0)
    rs_second(0, 0, 1)
    ag_forward(1, 1)
    ag_finish(1, 1)

    def step_out(r, at):
        gu_ref[:, at] = u_sum[:, at] + to_users(1, r)

    loop_users(step_out)
    gi_ref[...] = pick[:, 0:half] + rs_finish(0, 0)


def shards(
    user_embed, item_embed, adj_tiles, tile_rows, tile_cols, tile_count,
    triple_users, triple_pos, triple_neg,
):
    n = lax.axis_size("user")
    h = n // 2
    features, user_dev = user_embed.shape
    item_dev = item_embed.shape[1]
    wide = 2 * item_dev
    trips = triple_users.shape[0]
    chunks = user_dev // wide
    rmat = dense_rows(adj_tiles, tile_rows, tile_cols, tile_count, user_dev, item_dev * n)
    vmem = pl.BlockSpec(memory_space=pltpu.VMEM)
    dma = pltpu.SemaphoreType.DMA
    most = 56 << 20 if rmat.size > 8 << 20 else 24 << 20
    return pl.pallas_call(
        functools.partial(main_kernel, n),
        out_shape=(
            jax.ShapeDtypeStruct((features, user_dev), F32),
            jax.ShapeDtypeStruct((features, item_dev), F32),
        ),
        in_specs=[vmem] * 6,
        out_specs=(vmem, vmem),
        scratch_shapes=[
            pltpu.VMEM((2, 2, h, features, item_dev), F32),
            pltpu.VMEM((2, h, features, item_dev), F32),
            pltpu.VMEM((2, h, features, item_dev), BF16),
            pltpu.VMEM((2, h, features, item_dev), BF16),
            pltpu.VMEM((3, 2, h, features, item_dev), BF16),
            pltpu.VMEM((features, user_dev), BF16),
            pltpu.VMEM((features, user_dev), F32),
            pltpu.VMEM((features, user_dev), BF16),
            pltpu.VMEM((features, user_dev), BF16),
            pltpu.VMEM((chunks, wide, trips), BF16),
            pltpu.VMEM((chunks, trips, wide), BF16),
            pltpu.VMEM((h, wide, trips), BF16),
            pltpu.VMEM((h, trips, wide), BF16),
            pltpu.VMEM((features, trips), F32),
            pltpu.VMEM((2 * features, trips), F32),
            pltpu.VMEM((features, item_dev), F32),
            pltpu.VMEM((3, trips, 128), jnp.int32),
            dma((2, 2)), dma((2, 2)), dma((2, h)), dma((2, h)),
            dma((3, h)), dma((3, h)), dma((3, h)), dma((3, h)),
        ],
        compiler_params=pltpu.CompilerParams(
            collective_id=0, has_side_effects=True, vmem_limit_bytes=most
        ),
    )(
        user_embed, item_embed,
        triple_users.reshape(1, trips), triple_pos.reshape(1, trips), triple_neg.reshape(1, trips),
        rmat,
    )


def solution(mesh):
    split = P(("parts", "user"))
    columns = P(None, ("parts", "user"))
    return jax.shard_map(
        shards,
        mesh=mesh,
        in_specs=(columns, columns, P(("parts", "user"), None, None)) + (split,) * 6,
        out_specs=(columns, columns),
        check_vma=False,
    )
```
